128 devices in a mesh: depth: 2 (over core), row: 8 (over z, x_hi), col: 8 (over y, x_lo).
Axes of the slice: x: 4 (x_hi: 2, x_lo: 2; x = x_hi * 2 + x_lo), y: 4, z: 4, core: 2. Of those that a mesh axis runs over, the one named last changes fastest.
Arguments:
- activations: bfloat16 [16384, 6144], P(('depth', 'row'), 'col'), may hold values from -6 to 6
- weight: bfloat16 [6144, 6144], P(('depth', 'row'), 'col'), may hold values from -0.109375 to 0.109375
- cotangent: bfloat16 [16384, 6144], P(('depth', 'row'), 'col'), may hold values from -6 to 6
Outputs:
- projected: bfloat16 [16384, 6144], P(('depth', 'row'), 'col')
- grad_input: bfloat16 [16384, 6144], P(('depth', 'row'), 'col')
- grad_weight: bfloat16 [6144, 6144], P(('depth', 'row'), 'col')
The draws below stay inside these ranges and needn't reach their ends.
All inputs are finite; a program needn't handle non-finite values.
Results may differ from the reference program's by a relative error of at most 0.019.
Values may be sent and summed in bfloat16 or wider, within the bound.
No kernel may reach another device: no remote copies, remote signals or barrier semaphores. Data moves between devices by JAX's collectives and lax.ppermute only.
A program may use at most 128 MiB of HBM per device.

```python
import math
import jax
import jax.numpy as jnp

D = 6144
TOK_DEV = 1024
TOKENS = 16384
N_DEPTH = 2
N_ROW = 8
N_COL = 8


def raised(drawn, stream_key, source, target, blocks, factor):
    owner, partner = [(jnp.arange(drawn.shape[position]) // (drawn.shape[position] // blocks)).reshape([-1 if axis == position else 1 for axis in range(drawn.ndim)]) for position in (source, target)]
    chosen = jax.random.permutation(stream_key, blocks)[partner]
    strong = (owner == chosen) | (owner == (partner + blocks // 2) % blocks)
    return jnp.where(strong, factor * drawn, drawn)


def shard_levels(key, shape, cuts, low, high):
    loudness, own = 1.0, jax.random.fold_in(key, 6)
    for axis_at, parts in cuts:
        draws = jnp.exp(jax.random.uniform(jax.random.fold_in(own, axis_at), (parts,), jnp.float32, low / len(cuts), high / len(cuts)))
        loudness = loudness * jnp.repeat(draws, shape[axis_at] // parts).reshape([-1 if axis == axis_at else 1 for axis in range(len(shape))])
    return loudness


def normal_values(rng, dims, deviation, reach, split=(), held_as=jnp.bfloat16):
    gain = shard_levels(rng, dims, split, -0.22, 0.18) if split else 1.0
    drawn = jax.random.normal(rng, dims, jnp.float32) * deviation * gain
    return jnp.minimum(jnp.maximum(drawn, -reach), reach).astype(held_as)


def bell_draw_with(own_key, dims, deviation, most, cuts, heavy, dtype=jnp.bfloat16):
    drawn = deviation * jax.random.normal(own_key, dims, jnp.float32)
    if cuts:
        drawn = drawn * shard_levels(own_key, dims, cuts, -0.22, 0.18)
    return jnp.clip(raised(drawn, jax.random.fold_in(own_key, 3), *heavy), -most, most).astype(dtype)


def setup_inputs(seed: int = 0) -> dict:
    streams_of = jax.random.split(jax.random.key(seed), 4)
    return {
        "activations": bell_draw_with(streams_of[0], (TOKENS, D), 1.0, 6.0, ((0, 16), (1, 8)), (0, 1, 16, 2.0)),
        "weight": bell_draw_with(streams_of[1], (D, D), D ** -0.5, 0.109375, ((0, 16), (1, 8)), (1, 0, 16, 2.0)),
        "cotangent": normal_values(streams_of[2], (TOKENS, D), 1.0, 6.0, ((0, 16), (1, 8))),
    }


def reference(activations, weight, cotangent):
    projected = jnp.dot(activations, weight, preferred_element_type=jnp.float32).astype(jnp.bfloat16)
    block = D // N_COL
    total_input = jnp.zeros((TOKENS, D), jnp.float32)
    for index in range(N_COL):
        cot_block = cotangent[:, index * block:(index + 1) * block]
        weight_block = weight[:, index * block:(index + 1) * block]
        partial_value = jnp.dot(cot_block, weight_block.T, preferred_element_type=jnp.float32).astype(jnp.bfloat16)
        total_input = total_input + partial_value.astype(jnp.float32)
    grad_input = total_input.astype(jnp.bfloat16)
    groups = N_DEPTH * N_ROW
    total_weight = jnp.zeros((D, D), jnp.float32)
    for index in range(groups):
        act_group = activations[index * TOK_DEV:(index + 1) * TOK_DEV]
        cot_group = cotangent[index * TOK_DEV:(index + 1) * TOK_DEV]
        partial_value = jnp.dot(act_group.T, cot_group, preferred_element_type=jnp.float32).astype(jnp.bfloat16)
        total_weight = total_weight + partial_value.astype(jnp.float32)
    grad_weight = (total_weight * (1.0 / math.sqrt(TOKENS))).astype(jnp.bfloat16)
    return (projected, grad_input, grad_weight)
```

```python
import math

import jax
import jax.numpy as jnp
from jax import lax
from jax.sharding import PartitionSpec as P

AXES = ("depth", "row", "col")
F32, BF16 = jnp.float32, jnp.bfloat16


def send(value, target):
    pairs = []
    for c in range(2):
        for z in range(4):
            for xh in range(2):
                for y in range(4):
                    for xl in range(2):
                        to = target(c, z, xh, y, xl)
                        if to is not None:
                            tc, tz, txh, ty, txl = to
                            dst = tc * 64 + (tz % 4 * 2 + txh % 2) * 8 + ty % 4 * 2 + txl % 2
                            pairs.append((c * 64 + (z * 2 + xh) * 8 + y * 2 + xl, dst))
    return lax.ppermute(value, AXES, pairs)


def to_core(c, z, xh, y, xl):
    return (1 - c, z, xh, y, xl)


def to_y(step):
    return lambda c, z, xh, y, xl: (c, z, xh, y + step, xl)


def to_z(step, only=None):
    def target(c, z, xh, y, xl):
        if only is not None and (z % 2 == xl) != only:
            return None
        return (c, z + step, xh, y, xl)

    return target


def to_x(step, holders):
    def target(c, z, xh, y, xl):
        if (z % 2 == xl) != holders:
            return None
        x = (2 * xh + xl + step) % 4
        return (c, z, x // 2, y, x % 2)

    return target


def to_xl(c, z, xh, y, xl):
    return (c, z, xh, y, 1 - xl)


def dot(a, b, dims):
    return lax.dot_general(a, b, (dims, ((), ())), preferred_element_type=F32)


def add(*terms):
    total = terms[0].astype(F32)
    for term in terms[1:]:
        total = total + term.astype(F32)
    return total.astype(BF16)


def put(buffer, value, row, col):
    return lax.dynamic_update_slice(buffer, value, (row, col))


def cut(value, row, col, rows, cols):
    return lax.dynamic_slice(value, (row, col), (rows, cols))


def per_device(activations, weight, cotangent):
    tok, blk = activations.shape
    half = tok // 2
    part = weight.shape[0]
    c = lax.axis_index("depth")
    row, col = lax.axis_index("row"), lax.axis_index("col")
    z, xh, y, xl = row // 2, row % 2, col // 2, col % 2
    holder = z % 2 == xl
    zero = jnp.int32(0)

    def slot(block):
        block = block % 4
        return jnp.where(block // 2 == c, 0, 2) + block % 2

    g_other = send(cotangent, to_xl)
    g_full = jnp.concatenate([cotangent, g_other], axis=1)

    from_lo = send(weight, to_x(1, False))
    from_hi = send(weight, to_x(-1, False))
    from_opp = send(weight, to_x(2, True))
    near = jnp.where(xl == 0, from_hi, from_lo)
    far = jnp.where(xl == 0, from_lo, from_hi)
    up0 = send(weight, to_z(1))
    dn0 = send(weight, to_z(-1))
    up1 = send(jnp.where(holder, near, up0), to_z(1))
    dn1 = send(jnp.where(holder, far, dn0), to_z(-1))
    up2 = send(jnp.where(holder, far, up1), to_z(1))
    dn2 = send(jnp.where(holder, from_opp, dn1), to_z(-1))
    up3 = send(from_opp, to_z(1, True))
    dn3 = send(jnp.where(holder, near, dn2), to_z(-1))
    first = [
        jnp.where(holder, weight, up0),
        jnp.where(holder, near, up1),
        jnp.where(holder, far, up2),
        jnp.where(holder, from_opp, up3),
    ]
    second = [
        jnp.where(holder, up1, dn0),
        jnp.where(holder, up2, dn3),
        jnp.where(holder, dn2, dn1),
        jnp.where(holder, dn3, dn2),
    ]
    j_first = jnp.where(holder, z, (z + 3) % 4) // 2
    w_own = jnp.zeros((2 * blk, 2 * blk), BF16)
    own_row, opp_row = xh * part, (1 - xh) * part
    for j, tiles in ((j_first, first), (1 - j_first, second)):
        for tile, at, column in (
            (tiles[0], own_row, 0),
            (tiles[1], own_row, blk),
            (tiles[2], opp_row, blk),
            (tiles[3], opp_row, 0),
        ):
            w_own = put(w_own, tile, j * blk + at, zero + column)
    w_other = send(w_own, to_core)

    a_u, a_v = activations[:half], activations[half:]
    up_u = send(a_u, to_y(1))
    dn_v = send(a_v, to_y(-1))
    up_v = send(a_v, to_y(1))
    dn_u = send(a_u, to_y(-1))
    opp_u = send(up_u, to_y(1))
    opp_v = send(dn_v, to_y(-1))
    a_all = jnp.zeros((tok, 4 * blk), BF16)
    for block, top, bottom in (
        (y, a_u, a_v),
        (y + 3, up_u, up_v),
        (y + 1, dn_u, dn_v),
        (y + 2, opp_u, opp_v),
    ):
        at = slot(block) * blk
        a_all = put(a_all, top, zero, at)
        a_all = put(a_all, bottom, zero + half, at)
    a_cross = send(a_all[:, 2 * blk:], to_core)
    g_cross = send(g_full, to_core)

    d_all = jnp.concatenate(
        [dot(g_full, w_own, ((1,), (1,))).astype(BF16), dot(g_full, w_other, ((1,), (1,))).astype(BF16)],
        axis=1,
    )

    def d_block(block, first, rows):
        return cut(d_all, zero + first, slot(block) * blk, rows, blk)

    up0 = send(d_block(y + 2, 0, half), to_y(1))
    dn0 = send(d_block(y + 2, half, half), to_y(-1))
    up1 = send(d_block(y + 1, half, half), to_y(1))
    dn1 = send(d_block(y + 3, 0, half), to_y(-1))
    up2 = send(add(d_block(y + 1, 0, half), up0), to_y(1))
    dn2 = send(add(d_block(y + 3, half, half), dn0), to_y(-1))
    grad_input = jnp.concatenate(
        [add(d_block(y, 0, half), up2, dn1), add(d_block(y, half, half), up1, dn2)], axis=0
    )

    a_both = jnp.concatenate([a_all[:, : 2 * blk], a_cross], axis=0)
    g_both = jnp.concatenate([g_full, g_cross], axis=0)
    w_grad = dot(a_both, g_both, ((0,), (0,))).astype(BF16)

    def w_half(j, a):
        return cut(w_grad, j * blk + a * part, zero, part, 2 * blk)

    j_up = jnp.where(holder, (z + 2) % 4, (z + 1) % 4) // 2
    j_dn = jnp.where(holder, (z + 2) % 4, (z + 3) % 4) // 2
    lo, hi = jnp.where(holder, 0, 1), jnp.where(holder, 1, 0)
    up0 = send(w_half(j_up, lo), to_z(1))
    dn0 = send(w_half(j_dn, hi), to_z(-1))
    up1 = send(add(w_half(j_up, 0), up0), to_z(1, False))
    dn1 = send(add(w_half(j_dn, 1), dn0), to_z(-1, False))
    j_own = z // 2
    kept = jnp.concatenate(
        [add(w_half(j_own, 0), up1, dn0), add(w_half(j_own, 1), up0, dn1)], axis=0
    )
    near_tile = cut(kept, own_row, zero + blk, part, blk)
    far_tile = cut(kept, opp_row, zero + blk, part, blk)
    opp_tile = cut(kept, opp_row, zero, part, blk)
    own_tile = cut(kept, own_row, zero, part, blk)
    to_hi = jnp.where(xl == 0, near_tile, far_tile)
    to_lo = jnp.where(xl == 0, far_tile, near_tile)
    got_lo = send(to_hi, to_x(1, True))
    got_hi = send(to_lo, to_x(-1, True))
    got_opp = send(opp_tile, to_x(2, True))
    scaling = 1.0 / math.sqrt(tok * 16)
    total = jnp.where(
        holder,
        own_tile.astype(F32) + got_opp.astype(F32),
        got_lo.astype(F32) + got_hi.astype(F32),
    )
    grad_weight = (total * scaling).astype(BF16)

    w_all = jnp.concatenate([w_own, w_other], axis=0)
    p_other = send(dot(a_all, w_all[:, blk:], ((1,), (0,))).astype(BF16), to_xl)
    projected = (dot(a_all, w_all[:, :blk], ((1,), (0,))) + p_other.astype(F32)).astype(BF16)
    return (projected, grad_input, grad_weight)


def solution(mesh):
    spec = P(("depth", "row"), "col")
    return jax.shard_map(
        per_device, mesh=mesh, in_specs=(spec,) * 3, out_specs=(spec,) * 3, check_vma=False
    )
```

```python
import math

import jax
import jax.numpy as jnp
from jax import lax
from jax.experimental import pallas as pl
from jax.experimental.pallas import tpu as pltpu
from jax.sharding import PartitionSpec as P

AXES = ("depth", "row", "col")
F32, BF16 = jnp.float32, jnp.bfloat16


def send(value, target):
    pairs = []
    for c in range(2):
        for z in range(4):
            for xh in range(2):
                for y in range(4):
                    for xl in range(2):
                        to = target(c, z, xh, y, xl)
                        if to is not None:
                            tc, tz, txh, ty, txl = to
                            dst = tc * 64 + (tz % 4 * 2 + txh % 2) * 8 + ty % 4 * 2 + txl % 2
                            pairs.append((c * 64 + (z * 2 + xh) * 8 + y * 2 + xl, dst))
    return lax.ppermute(value, AXES, pairs)


def to_core(c, z, xh, y, xl):
    return (1 - c, z, xh, y, xl)


def to_y(step):
    return lambda c, z, xh, y, xl: (c, z, xh, y + step * (1 - 2 * c), xl)


def to_z(holders, others):
    def target(c, z, xh, y, xl):
        step = holders if z % 2 == xl else others
        return None if step is None else (c, z + step * (1 - 2 * c), xh, y, xl)

    return target


def to_x(step, holders):
    def target(c, z, xh, y, xl):
        if (z % 2 == xl) != holders:
            return None
        x = (2 * xh + xl + step) % 4
        return (c, z, x // 2, y, x % 2)

    return target


def to_xl(c, z, xh, y, xl):
    return (c, z, xh, y, 1 - xl)


def dot(a, b, dims):
    return lax.dot_general(a, b, (dims, ((), ())), preferred_element_type=F32)


def add(*terms):
    total = terms[0].astype(F32)
    for term in terms[1:]:
        total = total + term.astype(F32)
    return total.astype(BF16)


def after(value, *others):
    return lax.optimization_barrier((value,) + others)[0]


def put(buffer, value, row, col):
    return lax.dynamic_update_slice(buffer, value, (row, col))


def cut(value, row, col, rows, cols):
    return lax.dynamic_slice(value, (row, col), (rows, cols))


VMEM = pl.BlockSpec(memory_space=pltpu.VMEM)
SMEM = pl.BlockSpec(memory_space=pltpu.SMEM)
ANY = pl.BlockSpec(memory_space=pl.ANY)
LIMIT = 40 * 2**20


def stack(top, same, opposite, turn, from_hi, from_lo):
    rows, cols = same.shape

    def kernel(places_ref, *refs):
        for pair in range(2):
            one_ref, two_ref = refs[2 * pair: 2 * pair + 2]
            for value in range(2):

                @pl.when(places_ref[pair] == value)
                def _():
                    refs[4][pair, pl.ds(value * rows, rows), :] = one_ref[...]
                    refs[4][pair, pl.ds((1 - value) * rows, rows), :] = two_ref[...]

    return pl.pallas_call(
        kernel,
        out_shape=jax.ShapeDtypeStruct((2, 2 * rows, cols), same.dtype),
        in_specs=[SMEM] + [VMEM] * 4,
        out_specs=VMEM,
        compiler_params=pltpu.CompilerParams(vmem_limit_bytes=LIMIT),
        cost_estimate=pl.CostEstimate(flops=0, bytes_accessed=16 * rows * cols, transcendentals=0),
        name="stack",
    )(jnp.stack([top, turn]), same, opposite, from_hi, from_lo)


def input_term(which, g_own, g_other, weights):
    tok, blk = g_own.shape
    _, rows, _ = weights[0].shape
    step = tok // 4
    n = len(weights)

    def kernel(which_ref, g_own_ref, g_other_ref, *refs):
        out_ref, held, sem = refs[n:]

        @pl.when(pl.program_id(0) == 0)
        def _():
            for place in range(n):

                @pl.when(which_ref[0] == place)
                def _():
                    copy = pltpu.make_async_copy(refs[place], held, sem)
                    copy.start()
                    copy.wait()

        total = dot(g_own_ref[...], held[0], ((1,), (1,)))
        total += dot(g_other_ref[...], held[1], ((1,), (1,)))
        out_ref[...] = total.astype(BF16)

    g_spec = pl.BlockSpec((step, blk), lambda i: (i, 0))
    return pl.pallas_call(
        kernel,
        grid=(4,),
        out_shape=jax.ShapeDtypeStruct((tok, rows), BF16),
        in_specs=[SMEM, g_spec, g_spec] + [ANY] * n,
        out_specs=pl.BlockSpec((step, rows), lambda i: (i, 0)),
        scratch_shapes=[pltpu.VMEM((2, rows, blk), BF16), pltpu.SemaphoreType.DMA],
        compiler_params=pltpu.CompilerParams(vmem_limit_bytes=LIMIT),
        cost_estimate=pl.CostEstimate(
            flops=4 * tok * rows * blk, bytes_accessed=4 * (rows * blk + 2 * tok * blk), transcendentals=0
        ),
        name="input_term",
    )(jnp.reshape(which, (1,)), g_own, g_other, *weights)


def project(a_all, weights, part, dtype):
    tok, depth = a_all.shape
    _, blk, cols = weights[0].shape
    step = tok // 4
    n = len(weights)

    def kernel(a_ref, *refs):
        out_ref = refs[n]
        total = dot(a_ref[:, :blk], refs[0][0], ((1,), (0,)))
        for k in range(1, n):
            total += dot(a_ref[:, k * blk:(k + 1) * blk], refs[k][0], ((1,), (0,)))
        out_ref[...] = total.astype(dtype)

    return pl.pallas_call(
        kernel,
        grid=(4,),
        out_shape=jax.ShapeDtypeStruct((tok, cols), dtype),
        in_specs=[pl.BlockSpec((step, depth), lambda i: (i, 0))]
        + [pl.BlockSpec((1, blk, cols), lambda i: (part, 0, 0))] * n,
        out_specs=pl.BlockSpec((step, cols), lambda i: (i, 0)),
        compiler_params=pltpu.CompilerParams(vmem_limit_bytes=LIMIT),
        cost_estimate=pl.CostEstimate(
            flops=2 * tok * depth * cols, bytes_accessed=2 * depth * (tok + cols), transcendentals=0
        ),
        name="project",
    )(a_all, *weights)


def per_device(activations, weight, cotangent):
    tok, blk = activations.shape
    part = weight.shape[0]
    c = lax.axis_index("depth")
    row, col = lax.axis_index("row"), lax.axis_index("col")
    z, xh, y, xl = row >> 1, row & 1, col >> 1, col & 1
    holder = (z & 1) == xl
    zero = jnp.int32(0)
    sign = 1 - 2 * c

    def first_of(core):
        return (jnp.where(holder, z, z + 2 * core - 1) & 3) >> 1

    def slot(block):
        block = block & 3
        core = block >> 1
        return jnp.where(core == c, 0, 2) + jnp.where((block & 1) == first_of(core), 0, 1)

    half = tok // 2
    from_opp = send(weight, to_x(2, True))
    from_lo = send(weight, to_x(1, False))
    from_hi = send(weight, to_x(-1, False))
    a_behind = send(activations, to_y(1))
    g_upper, g_lower = cotangent[:half], cotangent[half:]
    from_opp, from_lo, from_hi, a_behind, act, g_upper, g_own = lax.optimization_barrier(
        (from_opp, from_lo, from_hi, a_behind, activations, g_upper, cotangent)
    )
    block = stack(xh, weight, from_opp, xh ^ xl, from_hi, from_lo)
    w_z = send(block, to_z(1, None))
    a_ahead = send(act, to_y(-1))
    g_upper = send(g_upper, to_xl)
    g_own_x = send(g_own, to_core)
    a_ahead, w_z, g_upper, g_own_x, a_relay, g_lower = lax.optimization_barrier(
        (a_ahead, w_z, g_upper, g_own_x, a_behind, g_lower)
    )
    w_first = jnp.where(holder, block, w_z)
    w_second = send(w_first, to_z(-1, 1))
    a_opp = send(a_relay, to_y(1))
    g_lower = send(g_lower, to_xl)
    w_first_x = send(w_first, to_core)
    w_second, a_opp, g_lower, w_first_x = lax.optimization_barrier(
        (w_second, a_opp, g_lower, w_first_x)
    )
    g_other = jnp.concatenate([g_upper, g_lower])

    a_all = after(jnp.zeros((tok, 4 * blk), BF16), from_lo)
    for which, value in ((y, activations), (y - sign, a_behind), (y + sign, a_ahead), (y + 2, a_opp)):
        a_all = put(a_all, value, zero, slot(which) * blk)
    a_cross = send(a_all[:, 2 * blk:], to_core)
    g_other_x = send(g_other, to_core)
    weights = [w_first, w_second, w_first_x, send(w_second, to_core)]

    a_own = a_all[:, : 2 * blk]

    def weight_term(g, g_x):
        total = dot(a_own, g, ((0,), (0,))) + dot(a_cross, g_x, ((0,), (0,)))
        return total.astype(BF16)

    wg_own = weight_term(cotangent, g_own_x)
    wg_other = weight_term(g_other, g_other_x)
    wg_own_s = jnp.where(holder, wg_own[blk:], wg_own[:blk])
    wg_other_s = jnp.where(holder, wg_other[blk:], wg_other[:blk])
    wg_own_a = send(wg_own_s, to_z(1, -1))
    wg_other_a = send(wg_other_s, to_z(1, -1))

    w_then = [after(weights[0], wg_own_s, wg_other_s)] + weights[1:]
    p_term = project(a_all, w_then, 1, BF16)
    p_other = send(p_term, to_xl)

    def d_block(which, *before):
        return input_term(slot(which), after(cotangent, *before), g_other, weights)

    d_opp = d_block(y + 2, p_term)
    d_a = send(d_opp, to_y(1))
    wg_own_t = add(wg_own[blk:], after(wg_own_a, d_opp))
    wg_own_b = send(wg_own_t, to_z(None, 1))
    d_behind = d_block(y - sign, wg_own_t)
    d_b = send(after(d_behind, d_a), to_y(-1))
    wg_other_t = add(wg_other[blk:], after(wg_other_a, d_behind))
    wg_other_b = send(wg_other_t, to_z(None, 1))
    d_ahead = d_block(y + sign, wg_other_t)
    d_own = d_block(y, d_ahead)
    d_c_term = add(after(d_ahead, d_own), after(d_a, d_b))
    d_c = send(d_c_term, to_y(1))

    kept_own = add(wg_own[:blk], wg_own_a, wg_own_b)
    got_opp = send(after(cut(kept_own, (1 - xh) * part, zero, part, blk), p_other), to_x(2, True))
    own_tile = cut(kept_own, xh * part, zero, part, blk)
    kept_other = add(wg_other[:blk], wg_other_a, wg_other_b)
    up = xh ^ xl
    got_lo = send(cut(kept_other, up * part, zero, part, blk), to_x(1, True))
    got_hi = send(cut(kept_other, (1 - up) * part, zero, part, blk), to_x(-1, True))

    w_then = [after(weights[0], d_own)] + weights[1:]
    p_own = project(a_all, w_then, 0, F32)
    projected = (p_own + p_other.astype(F32)).astype(BF16)
    got_lo, got_hi = after(got_lo, projected), after(got_hi, projected)
    grad_input = add(d_own, d_b, d_c)
    scaling = 1.0 / math.sqrt(tok * lax.axis_size("depth") * lax.axis_size("row"))
    total = jnp.where(
        holder,
        own_tile.astype(F32) + got_opp.astype(F32),
        got_lo.astype(F32) + got_hi.astype(F32),
    )
    grad_weight = (total * scaling).astype(BF16)
    return (projected, grad_input, grad_weight)


def solution(mesh):
    spec = P(("depth", "row"), "col")
    return jax.shard_map(
        per_device, mesh=mesh, in_specs=(spec,) * 3, out_specs=(spec,) * 3, check_vma=False
    )
```

```python
import math

import jax
import jax.numpy as jnp
from jax import lax
from jax.experimental import pallas as pl
from jax.experimental.pallas import tpu as pltpu
from jax.sharding import PartitionSpec as P

AXES = ("depth", "row", "col")
F32, BF16 = jnp.float32, jnp.bfloat16


def send(value, target):
    pairs = []
    for c in range(2):
        for z in range(4):
            for xh in range(2):
                for y in range(4):
                    for xl in range(2):
                        to = target(c, z, xh, y, xl)
                        if to is not None:
                            tc, tz, txh, ty, txl = to
                            dst = tc * 64 + (tz % 4 * 2 + txh % 2) * 8 + ty % 4 * 2 + txl % 2
                            pairs.append((c * 64 + (z * 2 + xh) * 8 + y * 2 + xl, dst))
    return lax.ppermute(value, AXES, pairs)


def to_core(c, z, xh, y, xl):
    return (1 - c, z, xh, y, xl)


def to_y(step):
    return lambda c, z, xh, y, xl: (c, z, xh, y + step * (1 - 2 * c), xl)


def to_z(holders, others):
    def target(c, z, xh, y, xl):
        step = holders if z % 2 == xl else others
        return None if step is None else (c, z + step * (1 - 2 * c), xh, y, xl)

    return target


def to_x(step, holders):
    def target(c, z, xh, y, xl):
        if (z % 2 == xl) != holders:
            return None
        x = (2 * xh + xl + step) % 4
        return (c, z, x // 2, y, x % 2)

    return target


def to_xl(c, z, xh, y, xl):
    return (c, z, xh, y, 1 - xl)


def dot(a, b, dims):
    return lax.dot_general(a, b, (dims, ((), ())), preferred_element_type=F32)


def add(*terms):
    total = terms[0].astype(F32)
    for term in terms[1:]:
        total = total + term.astype(F32)
    return total.astype(BF16)


def after(value, *others):
    return lax.optimization_barrier((value,) + others)[0]


def put(buffer, value, row, col):
    return lax.dynamic_update_slice(buffer, value, (row, col))


def cut(value, row, col, rows, cols):
    return lax.dynamic_slice(value, (row, col), (rows, cols))


VMEM = pl.BlockSpec(memory_space=pltpu.VMEM)
SMEM = pl.BlockSpec(memory_space=pltpu.SMEM)
ANY = pl.BlockSpec(memory_space=pl.ANY)
HBM = pl.BlockSpec(memory_space=pltpu.HBM)
LIMIT = 40 * 2**20


def local(kernel, out_shape, in_specs, out_spec, moved, name, aliases=None, scratch=()):
    return pl.pallas_call(
        kernel,
        out_shape=jax.ShapeDtypeStruct(out_shape, BF16),
        in_specs=in_specs,
        out_specs=out_spec,
        scratch_shapes=scratch,
        input_output_aliases=aliases or {},
        compiler_params=pltpu.CompilerParams(vmem_limit_bytes=LIMIT),
        cost_estimate=pl.CostEstimate(flops=0, bytes_accessed=moved, transcendentals=0),
        name=name,
    )


def stack(xl, from_lo, from_hi, from_opp):
    rows, cols = from_lo.shape

    def kernel(xl_ref, lo_ref, hi_ref, opp_ref, out_ref):
        for value, (near, far) in enumerate(((hi_ref, lo_ref), (lo_ref, hi_ref))):

            @pl.when(xl_ref[0] == value)
            def _():
                out_ref[0] = near[...]
                out_ref[1] = far[...]

        out_ref[2] = opp_ref[...]

    call = local(kernel, (3, rows, cols), [SMEM] + [VMEM] * 3, VMEM, 12 * rows * cols, "stack")
    return call(jnp.reshape(xl, (1,)), from_lo, from_hi, from_opp)


def choose(first, one, two):
    def kernel(first_ref, one_ref, two_ref, out_ref, sem):
        @pl.when(first_ref[0] == 1)
        def _():
            copy = pltpu.make_async_copy(one_ref, out_ref, sem)
            copy.start()
            copy.wait()

    call = local(
        kernel, one.shape, [SMEM, HBM, HBM], HBM, 4 * one.size, "choose", {2: 0}, (pltpu.SemaphoreType.DMA,)
    )
    return call(jnp.reshape(first.astype(jnp.int32), (1,)), one, two)


def assemble(xh, own, three):
    rows, cols = own.shape

    def kernel(xh_ref, own_ref, three_ref, out_ref):
        for value in range(2):
            upper = pl.ds(value * rows, rows)
            lower = pl.ds((1 - value) * rows, rows)

            @pl.when(xh_ref[0] == value)
            def _():
                out_ref[0, upper, :] = own_ref[...]
                out_ref[0, lower, :] = three_ref[2]
                out_ref[1, upper, :] = three_ref[0]
                out_ref[1, lower, :] = three_ref[1]

    call = local(kernel, (2, 2 * rows, cols), [SMEM, VMEM, VMEM], VMEM, 16 * rows * cols, "assemble")
    return call(jnp.reshape(xh, (1,)), own, three)


def row_halves(step, cols):
    return [
        pl.BlockSpec((step, cols), lambda i: (jnp.minimum(i, 1), 0)),
        pl.BlockSpec((step, cols), lambda i: (jnp.maximum(i - 2, 0), 0)),
    ]


def in_turn(upper_ref, lower_ref):
    return jnp.where(pl.program_id(0) < 2, upper_ref[...], lower_ref[...])


def input_term(which, g_own, g_other, weights):
    tok, blk = g_own.shape
    _, rows, _ = weights[0].shape
    step = tok // 4
    n = len(weights)

    def kernel(which_ref, g_own_ref, upper_ref, lower_ref, *refs):
        out_ref, held, sem = refs[n:]

        @pl.when(pl.program_id(0) == 0)
        def _():
            for place in range(n):

                @pl.when(which_ref[0] == place)
                def _():
                    copy = pltpu.make_async_copy(refs[place], held, sem)
                    copy.start()
                    copy.wait()

        total = dot(g_own_ref[...], held[0], ((1,), (1,)))
        total += dot(in_turn(upper_ref, lower_ref), held[1], ((1,), (1,)))
        out_ref[...] = total.astype(BF16)

    g_spec = pl.BlockSpec((step, blk), lambda i: (i, 0))
    return pl.pallas_call(
        kernel,
        grid=(4,),
        out_shape=jax.ShapeDtypeStruct((tok, rows), BF16),
        in_specs=[SMEM, g_spec] + row_halves(step, blk) + [ANY] * n,
        out_specs=pl.BlockSpec((step, rows), lambda i: (i, 0)),
        scratch_shapes=[pltpu.VMEM((2, rows, blk), BF16), pltpu.SemaphoreType.DMA],
        compiler_params=pltpu.CompilerParams(vmem_limit_bytes=LIMIT),
        cost_estimate=pl.CostEstimate(
            flops=4 * tok * rows * blk, bytes_accessed=4 * (rows * blk + 2 * tok * blk), transcendentals=0
        ),
        name="input_term",
    )(jnp.reshape(which, (1,)), g_own, *g_other, *weights)


def project(a_all, weights, places, part, dtype, start, first=0, steps=4):
    tok, depth = a_all.shape
    _, blk, cols = weights[places[0]].shape
    step = tok // 4
    n = len(places)

    def kernel(a_ref, *refs):
        if len(start) == 2:
            total = in_turn(*refs[n: n + 2]).astype(F32)
        else:
            total = refs[n][...].astype(F32) if start else None
        for k, place in enumerate(places):
            term = dot(a_ref[:, place * blk:(place + 1) * blk], refs[k][0], ((1,), (0,)))
            total = term if total is None else total + term
        refs[-1][...] = total.astype(dtype)

    start_specs = row_halves(step, cols) if len(start) == 2 else [
        pl.BlockSpec((step, cols), lambda i: (first + i, 0))
    ] * len(start)
    return pl.pallas_call(
        kernel,
        grid=(steps,),
        out_shape=jax.ShapeDtypeStruct((steps * step, cols), dtype),
        in_specs=[pl.BlockSpec((step, depth), lambda i: (first + i, 0))]
        + [pl.BlockSpec((1, blk, cols), lambda i: (part, 0, 0))] * n
        + start_specs,
        out_specs=pl.BlockSpec((step, cols), lambda i: (i, 0)),
        compiler_params=pltpu.CompilerParams(vmem_limit_bytes=LIMIT),
        cost_estimate=pl.CostEstimate(
            flops=2 * steps * step * n * blk * cols, bytes_accessed=2 * n * blk * (tok + cols), transcendentals=0
        ),
        name="project",
    )(a_all, *(weights[place] for place in places), *start)


def per_device(activations, weight, cotangent):
    tok, blk = activations.shape
    part = weight.shape[0]
    c = lax.axis_index("depth")
    row, col = lax.axis_index("row"), lax.axis_index("col")
    z, xh, y, xl = row >> 1, row & 1, col >> 1, col & 1
    holder = (z & 1) == xl
    zero = jnp.int32(0)
    sign = 1 - 2 * c

    def first_of(core):
        return (jnp.where(holder, z, z + 2 * core - 1) & 3) >> 1

    def slot(block):
        block = block & 3
        core = block >> 1
        return jnp.where(core == c, 0, 2) + jnp.where((block & 1) == first_of(core), 0, 1)

    half = tok // 2
    from_opp = send(weight, to_x(2, True))
    from_lo = send(weight, to_x(1, False))
    from_hi = send(weight, to_x(-1, False))
    a_behind = send(activations, to_y(1))
    own_z = send(weight, to_z(1, None))
    own_first = jnp.where(holder, weight, after(own_z, from_opp))
    own_second = send(own_first, to_z(-1, 1))
    g_upper, g_lower = cotangent[:half], cotangent[half:]
    from_opp, from_lo, from_hi, a_behind, own_first, own_second, g_upper, act = lax.optimization_barrier(
        (from_opp, from_lo, from_hi, a_behind, own_first, own_second, g_upper, activations)
    )
    three = stack(xl, from_lo, from_hi, from_opp)
    three_z = send(three, to_z(1, None))
    a_ahead = send(act, to_y(-1))
    g_upper = send(g_upper, to_xl)
    a_all = after(jnp.zeros((tok, 4 * blk), BF16), from_lo)
    a_all = put(a_all, activations, zero, slot(y) * blk)
    a_all = put(a_all, a_behind, zero, slot(y - sign) * blk)
    three_z, a_ahead, g_upper, g_lower, a_relay = lax.optimization_barrier(
        (three_z, a_ahead, g_upper, g_lower, a_behind)
    )
    three_first = choose(holder, three, three_z)
    three_second = send(three_first, to_z(-1, 1))
    a_opp = send(a_relay, to_y(1))
    g_lower = send(g_lower, to_xl)
    w_first = assemble(xh, own_first, three_first)
    w_first_x = send(w_first, to_core)
    a_all = put(a_all, a_ahead, zero, slot(y + sign) * blk)
    three_second, a_opp, g_lower, w_first_x, a_all = lax.optimization_barrier(
        (three_second, a_opp, g_lower, w_first_x, a_all)
    )
    w_second = assemble(xh, own_second, three_second)
    w_second_x = send(w_second, to_core)
    weights = [w_first, w_second, w_first_x, w_second_x]
    a_all = put(a_all, after(a_opp, w_second), zero, slot(y + 2) * blk)

    def weight_term(first, g):
        return dot(a_all[:, first * blk:(first + 2) * blk], g, ((0,), (0,)))

    wg_own_x = send(weight_term(2, cotangent).astype(BF16), to_core)
    wg_own = weight_term(0, cotangent)
    g_other = jnp.concatenate([g_upper, g_lower])
    wg_other_x = send(weight_term(2, after(g_other, wg_own)).astype(BF16), to_core)
    wg_other = weight_term(0, g_other)
    wg_own = (wg_own + wg_own_x.astype(F32)).astype(BF16)
    wg_own_s = jnp.where(holder, wg_own[blk:], wg_own[:blk])
    wg_own_a = send(wg_own_s, to_z(1, -1))

    def d_block(which, *before):
        return input_term(slot(which), after(cotangent, *before), (g_upper, g_lower), weights)

    d_opp = d_block(y + 2, wg_other)
    d_a = send(d_opp, to_y(1))
    w_then = [after(w_first, d_opp), w_second, w_first_x, w_second_x]
    p_term = project(a_all, w_then, (0, 1, 2, 3), 1, BF16, ())
    p_other = send(p_term, to_xl)
    wg_other = (wg_other + after(wg_other_x, d_opp).astype(F32)).astype(BF16)
    wg_other_s = jnp.where(holder, wg_other[blk:], wg_other[:blk])
    wg_other_a = send(wg_other_s, to_z(1, -1))
    wg_own_t = add(wg_own[blk:], after(wg_own_a, p_term))
    wg_own_b = send(wg_own_t, to_z(None, 1))
    d_behind = after(d_block(y - sign, wg_own_t), d_a)
    d_b = send(d_behind, to_y(-1))
    d_ahead = d_block(y + sign, d_behind)
    d_own = d_block(y, d_ahead)
    wg_other_t = add(wg_other[blk:], after(wg_other_a, d_own))
    wg_other_b = send(wg_other_t, to_z(None, 1))
    d_c_term = add(d_ahead, after(d_a, d_b, p_other))
    d_c = send(d_c_term, to_y(1))

    kept_own = add(wg_own[:blk], wg_own_a, wg_own_b)
    got_opp = send(after(cut(kept_own, (1 - xh) * part, zero, part, blk), p_other, d_c_term), to_x(2, True))
    own_tile = cut(kept_own, xh * part, zero, part, blk)
    kept_other = add(wg_other[:blk], wg_other_a, wg_other_b)
    up = xh ^ xl
    got_lo = send(cut(kept_other, up * part, zero, part, blk), to_x(1, True))
    got_hi = send(cut(kept_other, (1 - up) * part, zero, part, blk), to_x(-1, True))

    w_then = [after(weights[0], d_own)] + weights[1:]
    projected = project(a_all, w_then, (0, 1, 2, 3), 0, BF16, (p_other,))
    got_lo, got_hi = after(got_lo, projected), after(got_hi, projected)
    grad_input = add(d_own, d_b, d_c)
    scaling = 1.0 / math.sqrt(tok * lax.axis_size("depth") * lax.axis_size("row"))
    total = jnp.where(
        holder,
        own_tile.astype(F32) + got_opp.astype(F32),
        got_lo.astype(F32) + got_hi.astype(F32),
    )
    grad_weight = (total * scaling).astype(BF16)
    return (projected, grad_input, grad_weight)


def solution(mesh):
    spec = P(("depth", "row"), "col")
    return jax.shard_map(
        per_device, mesh=mesh, in_specs=(spec,) * 3, out_specs=(spec,) * 3, check_vma=False
    )
```

```python
import math

import jax
import jax.numpy as jnp
from jax import lax
from jax.experimental import pallas as pl
from jax.experimental.pallas import tpu as pltpu
from jax.sharding import PartitionSpec as P

AXES = ("depth", "row", "col")
F32, BF16 = jnp.float32, jnp.bfloat16


def send(value, target):
    pairs = []
    for c in range(2):
        for z in range(4):
            for xh in range(2):
                for y in range(4):
                    for xl in range(2):
                        to = target(c, z, xh, y, xl)
                        if to is not None:
                            tc, tz, txh, ty, txl = to
                            dst = tc * 64 + (tz % 4 * 2 + txh % 2) * 8 + ty % 4 * 2 + txl % 2
                            pairs.append((c * 64 + (z * 2 + xh) * 8 + y * 2 + xl, dst))
    return lax.ppermute(value, AXES, pairs)


def to_core(c, z, xh, y, xl):
    return (1 - c, z, xh, y, xl)


def to_y(step):
    return lambda c, z, xh, y, xl: (c, z, xh, y + step * (1 - 2 * c), xl)


def to_z(holders, others):
    def target(c, z, xh, y, xl):
        step = holders if z % 2 == xl else others
        return None if step is None else (c, z + step * (1 - 2 * c), xh, y, xl)

    return target


def to_x(step, holders):
    def target(c, z, xh, y, xl):
        if (z % 2 == xl) != holders:
            return None
        x = (2 * xh + xl + step) % 4
        return (c, z, x // 2, y, x % 2)

    return target


def to_xl(c, z, xh, y, xl):
    return (c, z, xh, y, 1 - xl)


def dot(a, b, dims):
    return lax.dot_general(a, b, (dims, ((), ())), preferred_element_type=F32)


def add(*terms):
    total = terms[0].astype(F32)
    for term in terms[1:]:
        total = total + term.astype(F32)
    return total.astype(BF16)


def after(value, *others):
    return lax.optimization_barrier((value,) + others)[0]


def put(buffer, value, row, col):
    return lax.dynamic_update_slice(buffer, value, (row, col))


def cut(value, row, col, rows, cols):
    return lax.dynamic_slice(value, (row, col), (rows, cols))


VMEM = pl.BlockSpec(memory_space=pltpu.VMEM)
SMEM = pl.BlockSpec(memory_space=pltpu.SMEM)
ANY = pl.BlockSpec(memory_space=pl.ANY)
HBM = pl.BlockSpec(memory_space=pltpu.HBM)
LIMIT = 13 * 2**20


def local(kernel, out_shape, in_specs, out_spec, moved, name, aliases=None, scratch=()):
    return pl.pallas_call(
        kernel,
        out_shape=jax.ShapeDtypeStruct(out_shape, BF16),
        in_specs=in_specs,
        out_specs=out_spec,
        scratch_shapes=scratch,
        input_output_aliases=aliases or {},
        compiler_params=pltpu.CompilerParams(vmem_limit_bytes=LIMIT),
        cost_estimate=pl.CostEstimate(flops=0, bytes_accessed=moved, transcendentals=0),
        name=name,
    )


def stack(xl, from_lo, from_hi, from_opp):
    rows, cols = from_lo.shape

    def kernel(xl_ref, lo_ref, hi_ref, opp_ref, out_ref):
        for value, (near, far) in enumerate(((hi_ref, lo_ref), (lo_ref, hi_ref))):

            @pl.when(xl_ref[0] == value)
            def _():
                out_ref[0] = near[...]
                out_ref[1] = far[...]

        out_ref[2] = opp_ref[...]

    call = local(kernel, (3, rows, cols), [SMEM] + [VMEM] * 3, VMEM, 12 * rows * cols, "stack")
    return call(jnp.reshape(xl, (1,)), from_lo, from_hi, from_opp)


def choose(first, one, two):
    def kernel(first_ref, one_ref, two_ref, out_ref, sem):
        @pl.when(first_ref[0] == 1)
        def _():
            copy = pltpu.make_async_copy(one_ref, out_ref, sem)
            copy.start()
            copy.wait()

    call = local(
        kernel, one.shape, [SMEM, HBM, HBM], HBM, 4 * one.size, "choose", {2: 0}, (pltpu.SemaphoreType.DMA,)
    )
    return call(jnp.reshape(first.astype(jnp.int32), (1,)), one, two)


def assemble(xh, own, three):
    rows, cols = own.shape

    def kernel(xh_ref, own_ref, three_ref, out_ref, sem):
        for value in range(2):
            upper = pl.ds(value * rows, rows)
            lower = pl.ds((1 - value) * rows, rows)

            @pl.when(xh_ref[0] == value)
            def _():
                pairs = (
                    (own_ref, out_ref.at[0, upper]),
                    (three_ref.at[2], out_ref.at[0, lower]),
                    (three_ref.at[0], out_ref.at[1, upper]),
                    (three_ref.at[1], out_ref.at[1, lower]),
                )
                copies = [pltpu.make_async_copy(*pair, sem.at[k]) for k, pair in enumerate(pairs)]
                for copy in copies:
                    copy.start()
                for copy in copies:
                    copy.wait()

    call = local(
        kernel, (2, 2 * rows, cols), [SMEM, ANY, ANY], HBM, 16 * rows * cols, "assemble", None,
        (pltpu.SemaphoreType.DMA((4,)),)
    )
    return call(jnp.reshape(xh, (1,)), own, three)


def input_term(which, g_own, g_other, weights):
    tok, blk = g_own.shape
    _, rows, _ = weights[0].shape
    step = tok // 4
    n = len(weights)

    def kernel(which_ref, g_own_ref, upper_ref, lower_ref, *refs):
        out_ref, held, sem = refs[n:]
        half = pl.program_id(0) // 2

        @pl.when(pl.program_id(0) == 0)
        def _():
            for place in range(n):

                @pl.when(which_ref[0] == place)
                def _():
                    copy = pltpu.make_async_copy(refs[place], held, sem)
                    copy.start()
                    copy.wait()

        g_other_block = jnp.where(half == 0, upper_ref[...], lower_ref[...])
        total = dot(g_own_ref[...], held[0], ((1,), (1,)))
        total += dot(g_other_block, held[1], ((1,), (1,)))
        out_ref[...] = total.astype(BF16)

    g_spec = pl.BlockSpec((step, blk), lambda i: (i, 0))
    upper_spec = pl.BlockSpec((step, blk), lambda i: (jnp.minimum(i, 1), 0))
    lower_spec = pl.BlockSpec((step, blk), lambda i: (jnp.maximum(i - 2, 0), 0))
    return pl.pallas_call(
        kernel,
        grid=(4,),
        out_shape=jax.ShapeDtypeStruct((tok, rows), BF16),
        in_specs=[SMEM, g_spec, upper_spec, lower_spec] + [HBM] * n,
        out_specs=g_spec,
        scratch_shapes=[pltpu.VMEM((2, rows, blk), BF16), pltpu.SemaphoreType.DMA],
        compiler_params=pltpu.CompilerParams(vmem_limit_bytes=LIMIT),
        cost_estimate=pl.CostEstimate(
            flops=4 * tok * rows * blk, bytes_accessed=4 * (rows * blk + 2 * tok * blk), transcendentals=0
        ),
        name="input_term",
    )(jnp.reshape(which, (1,)), g_own, *g_other, *weights)


def project(a_all, weights, places, part, dtype, start=()):
    tok, depth = a_all.shape
    _, blk, cols = weights[places[0]].shape
    step = tok // 4
    n = len(places)

    def kernel(a_ref, *refs):
        out_ref, held, sem = refs[-3:]
        copies = [pltpu.make_async_copy(refs[k].at[part], held.at[k], sem.at[k]) for k in range(n)]

        @pl.when(pl.program_id(0) == 0)
        def _():
            for copy in copies:
                copy.start()
            for copy in copies:
                copy.wait()

        total = refs[n][...].astype(F32) if start else None
        for k, place in enumerate(places):
            term = dot(a_ref[:, place * blk:(place + 1) * blk], held[k], ((1,), (0,)))
            total = term if total is None else total + term
        out_ref[...] = total.astype(dtype)

    row_spec = pl.BlockSpec((step, cols), lambda i: (i, 0))
    return pl.pallas_call(
        kernel,
        grid=(4,),
        out_shape=jax.ShapeDtypeStruct((tok, cols), dtype),
        in_specs=[pl.BlockSpec((step, depth), lambda i: (i, 0))] + [HBM] * n + [row_spec] * len(start),
        out_specs=row_spec,
        scratch_shapes=[pltpu.VMEM((n, blk, cols), BF16), pltpu.SemaphoreType.DMA((n,))],
        compiler_params=pltpu.CompilerParams(vmem_limit_bytes=LIMIT),
        cost_estimate=pl.CostEstimate(
            flops=2 * tok * n * blk * cols, bytes_accessed=2 * n * blk * (tok + cols), transcendentals=0
        ),
        name="project",
    )(a_all, *(weights[place] for place in places), *start)


def per_device(activations, weight, cotangent):
    tok, blk = activations.shape
    part = weight.shape[0]
    c = lax.axis_index("depth")
    row, col = lax.axis_index("row"), lax.axis_index("col")
    z, xh, y, xl = row >> 1, row & 1, col >> 1, col & 1
    holder = (z & 1) == xl
    zero = jnp.int32(0)
    sign = 1 - 2 * c

    def first_of(core):
        return (jnp.where(holder, z, z + 2 * core - 1) & 3) >> 1

    def slot(block):
        block = block & 3
        core = block >> 1
        return jnp.where(core == c, 0, 2) + jnp.where((block & 1) == first_of(core), 0, 1)

    half = tok // 2
    from_opp = send(weight, to_x(2, True))
    from_lo = send(weight, to_x(1, False))
    from_hi = send(weight, to_x(-1, False))
    a_behind = send(activations, to_y(1))
    own_z = send(weight, to_z(1, None))
    own_first = jnp.where(holder, weight, after(own_z, from_opp))
    own_second = send(own_first, to_z(-1, 1))
    a_ahead = send(after(activations, from_opp, own_z), to_y(-1))
    g_upper, g_lower = cotangent[:half], cotangent[half:]
    from_opp, from_lo, from_hi, a_behind, own_first, own_second, g_upper = lax.optimization_barrier(
        (from_opp, from_lo, from_hi, a_behind, own_first, own_second, g_upper)
    )
    three = stack(xl, from_lo, from_hi, from_opp)
    three_z = send(three, to_z(1, None))
    a_opp = send(a_behind, to_y(1))
    g_upper = send(g_upper, to_xl)
    a_all = after(jnp.zeros((tok, 4 * blk), BF16), from_lo)
    for which, value in ((y, activations), (y - sign, a_behind), (y + sign, a_ahead), (y + 2, a_opp)):
        a_all = put(a_all, value, zero, slot(which) * blk)
    three_z, g_upper, g_lower, a_all = lax.optimization_barrier((three_z, g_upper, g_lower, a_all))

    def weight_term(first, g):
        return dot(a_all[:, first * blk:(first + 2) * blk], g, ((0,), (0,)))

    three_first = choose(holder, three, three_z)
    three_second = send(three_first, to_z(-1, 1))
    g_lower = send(g_lower, to_xl)
    w_first = assemble(xh, own_first, three_first)
    w_first_x = send(w_first, to_core)
    wg_own_x = weight_term(2, after(cotangent, w_first)).astype(BF16)
    wg_own = weight_term(0, after(cotangent, wg_own_x))
    p_part = project(a_all, [w_first, None, w_first_x], (0, 2), 1, F32, ())
    three_second, g_lower, w_first_x, wg_own_x, wg_own, p_part = lax.optimization_barrier(
        (three_second, g_lower, w_first_x, wg_own_x, wg_own, p_part)
    )
    w_second = assemble(xh, own_second, three_second)
    w_second_x = send(w_second, to_core)
    weights = [w_first, w_second, w_first_x, w_second_x]

    wg_own_x = send(wg_own_x, to_core)
    g_other = jnp.concatenate([g_upper, g_lower])
    wg_other_x = weight_term(2, after(g_other, w_second)).astype(BF16)
    wg_own = (wg_own + after(wg_own_x, wg_other_x).astype(F32)).astype(BF16)
    wg_other_x = send(wg_other_x, to_core)
    wg_own_s = jnp.where(holder, wg_own[blk:], wg_own[:blk])
    wg_own_a = send(wg_own_s, to_z(1, -1))

    def d_block(which, *before):
        return input_term(slot(which), after(cotangent, *before), (g_upper, g_lower), weights)

    w_then = [None, after(w_second, wg_own_s), None, w_second_x]
    p_term = project(a_all, w_then, (1, 3), 1, BF16, (p_part,))
    p_other = send(p_term, to_xl)

    d_opp = d_block(y + 2, p_term)
    d_a = send(d_opp, to_y(1))
    wg_other = weight_term(0, after(g_other, d_opp))
    wg_other = (wg_other + wg_other_x.astype(F32)).astype(BF16)
    wg_other_s = jnp.where(holder, wg_other[blk:], wg_other[:blk])
    wg_other_a = send(wg_other_s, to_z(1, -1))
    wg_own_t = add(wg_own[blk:], after(wg_own_a, wg_other_s))
    wg_own_b = send(wg_own_t, to_z(None, 1))
    d_behind = after(d_block(y - sign, wg_own_t), d_a)
    d_b = send(d_behind, to_y(-1))
    d_ahead = d_block(y + sign, d_behind)
    wg_other_t = add(wg_other[blk:], after(wg_other_a, d_ahead))
    wg_other_b = send(wg_other_t, to_z(None, 1))
    d_own = d_block(y, wg_other_t)
    d_c_term = add(d_ahead, after(d_a, d_b, p_other, d_own))
    d_c = send(d_c_term, to_y(1))

    kept_own = add(wg_own[:blk], wg_own_a, wg_own_b)
    opp_tile = after(cut(kept_own, (1 - xh) * part, zero, part, blk), p_other, d_c_term)
    got_opp = send(opp_tile, to_x(2, True))
    own_tile = cut(kept_own, xh * part, zero, part, blk)
    w_then = [after(weights[0], d_own, opp_tile)] + weights[1:]
    projected = project(a_all, w_then, (0, 1, 2, 3), 0, BF16, (p_other,))
    kept_other = add(wg_other[:blk], wg_other_a, after(wg_other_b, projected))
    up = xh ^ xl
    got_lo = send(cut(kept_other, up * part, zero, part, blk), to_x(1, True))
    got_hi = send(cut(kept_other, (1 - up) * part, zero, part, blk), to_x(-1, True))
    grad_input = add(d_own, d_b, after(d_c, got_opp))
    got_lo, got_hi = after(got_lo, grad_input), after(got_hi, grad_input)
    scaling = 1.0 / math.sqrt(tok * lax.axis_size("depth") * lax.axis_size("row"))
    total = jnp.where(
        holder,
        own_tile.astype(F32) + got_opp.astype(F32),
        got_lo.astype(F32) + got_hi.astype(F32),
    )
    grad_weight = (total * scaling).astype(BF16)
    return (projected, grad_input, grad_weight)


def solution(mesh):
    spec = P(("depth", "row"), "col")
    return jax.shard_map(
        per_device, mesh=mesh, in_specs=(spec,) * 3, out_specs=(spec,) * 3, check_vma=False
    )
```

```python
import math

import jax
import jax.numpy as jnp
from jax import lax
from jax.experimental import pallas as pl
from jax.experimental.pallas import tpu as pltpu
from jax.sharding import PartitionSpec as P

AXES = ("depth", "row", "col")
F32, BF16 = jnp.float32, jnp.bfloat16


def send(value, target):
    pairs = []
    for c in range(2):
        for z in range(4):
            for xh in range(2):
                for y in range(4):
                    for xl in range(2):
                        to = target(c, z, xh, y, xl)
                        if to is not None:
                            tc, tz, txh, ty, txl = to
                            dst = tc * 64 + (tz % 4 * 2 + txh % 2) * 8 + ty % 4 * 2 + txl % 2
                            pairs.append((c * 64 + (z * 2 + xh) * 8 + y * 2 + xl, dst))
    return lax.ppermute(value, AXES, pairs)


def to_core(c, z, xh, y, xl):
    return (1 - c, z, xh, y, xl)


def to_y(step):
    return lambda c, z, xh, y, xl: (c, z, xh, y + step * (1 - 2 * c), xl)


def to_z(holders, others):
    def target(c, z, xh, y, xl):
        step = holders if z % 2 == xl else others
        return None if step is None else (c, z + step * (1 - 2 * c), xh, y, xl)

    return target


def to_x(step, holders):
    def target(c, z, xh, y, xl):
        if (z % 2 == xl) != holders:
            return None
        x = (2 * xh + xl + step) % 4
        return (c, z, x // 2, y, x % 2)

    return target


def to_xl(c, z, xh, y, xl):
    return (c, z, xh, y, 1 - xl)


def dot(a, b, dims):
    return lax.dot_general(a, b, (dims, ((), ())), preferred_element_type=F32)


def add(*terms):
    total = terms[0].astype(F32)
    for term in terms[1:]:
        total = total + term.astype(F32)
    return total.astype(BF16)


def after(value, *others):
    return lax.optimization_barrier((value,) + others)[0]


def put(buffer, value, row, col):
    return lax.dynamic_update_slice(buffer, value, (row, col))


def cut(value, row, col, rows, cols):
    return lax.dynamic_slice(value, (row, col), (rows, cols))


VMEM = pl.BlockSpec(memory_space=pltpu.VMEM)
SMEM = pl.BlockSpec(memory_space=pltpu.SMEM)
ANY = pl.BlockSpec(memory_space=pl.ANY)
HBM = pl.BlockSpec(memory_space=pltpu.HBM)
LIMIT = 13 * 2**20


def local(kernel, out_shape, in_specs, out_spec, moved, name, aliases=None, scratch=()):
    return pl.pallas_call(
        kernel,
        out_shape=jax.ShapeDtypeStruct(out_shape, BF16),
        in_specs=in_specs,
        out_specs=out_spec,
        scratch_shapes=scratch,
        input_output_aliases=aliases or {},
        compiler_params=pltpu.CompilerParams(vmem_limit_bytes=LIMIT),
        cost_estimate=pl.CostEstimate(flops=0, bytes_accessed=moved, transcendentals=0),
        name=name,
    )


def stack(xl, from_lo, from_hi, from_opp):
    rows, cols = from_lo.shape

    def kernel(xl_ref, lo_ref, hi_ref, opp_ref, out_ref):
        for value, (near, far) in enumerate(((hi_ref, lo_ref), (lo_ref, hi_ref))):

            @pl.when(xl_ref[0] == value)
            def _():
                out_ref[0] = near[...]
                out_ref[1] = far[...]

        out_ref[2] = opp_ref[...]

    call = local(kernel, (3, rows, cols), [SMEM] + [VMEM] * 3, VMEM, 12 * rows * cols, "stack")
    return call(jnp.reshape(xl, (1,)), from_lo, from_hi, from_opp)


def choose(first, one, two):
    def kernel(first_ref, one_ref, two_ref, out_ref, sem):
        @pl.when(first_ref[0] == 1)
        def _():
            copy = pltpu.make_async_copy(one_ref, out_ref, sem)
            copy.start()
            copy.wait()

    call = local(
        kernel, one.shape, [SMEM, HBM, HBM], HBM, 4 * one.size, "choose", {2: 0}, (pltpu.SemaphoreType.DMA,)
    )
    return call(jnp.reshape(first.astype(jnp.int32), (1,)), one, two)


def assemble(xh, own, three):
    rows, cols = own.shape

    def kernel(xh_ref, own_ref, three_ref, out_ref, sem):
        for value in range(2):
            upper = pl.ds(value * rows, rows)
            lower = pl.ds((1 - value) * rows, rows)

            @pl.when(xh_ref[0] == value)
            def _():
                pairs = (
                    (own_ref, out_ref.at[0, upper]),
                    (three_ref.at[2], out_ref.at[0, lower]),
                    (three_ref.at[0], out_ref.at[1, upper]),
                    (three_ref.at[1], out_ref.at[1, lower]),
                )
                copies = [pltpu.make_async_copy(*pair, sem.at[k]) for k, pair in enumerate(pairs)]
                for copy in copies:
                    copy.start()
                for copy in copies:
                    copy.wait()

    call = local(
        kernel, (2, 2 * rows, cols), [SMEM, ANY, ANY], HBM, 16 * rows * cols, "assemble", None,
        (pltpu.SemaphoreType.DMA((4,)),)
    )
    return call(jnp.reshape(xh, (1,)), own, three)


def input_term(which, g_own, g_other, weights):
    tok, blk = g_own.shape
    _, rows, _ = weights[0].shape
    step = tok // 4
    n = len(weights)

    def kernel(which_ref, g_own_ref, upper_ref, lower_ref, *refs):
        out_ref, held, sem = refs[n:]
        half = pl.program_id(0) // 2

        @pl.when(pl.program_id(0) == 0)
        def _():
            for place in range(n):

                @pl.when(which_ref[0] == place)
                def _():
                    copy = pltpu.make_async_copy(refs[place], held, sem)
                    copy.start()
                    copy.wait()

        g_other_block = jnp.where(half == 0, upper_ref[...], lower_ref[...])
        total = dot(g_own_ref[...], held[0], ((1,), (1,)))
        total += dot(g_other_block, held[1], ((1,), (1,)))
        out_ref[...] = total.astype(BF16)

    g_spec = pl.BlockSpec((step, blk), lambda i: (i, 0))
    upper_spec = pl.BlockSpec((step, blk), lambda i: (jnp.minimum(i, 1), 0))
    lower_spec = pl.BlockSpec((step, blk), lambda i: (jnp.maximum(i - 2, 0), 0))
    return pl.pallas_call(
        kernel,
        grid=(4,),
        out_shape=jax.ShapeDtypeStruct((tok, rows), BF16),
        in_specs=[SMEM, g_spec, upper_spec, lower_spec] + [HBM] * n,
        out_specs=g_spec,
        scratch_shapes=[pltpu.VMEM((2, rows, blk), BF16), pltpu.SemaphoreType.DMA],
        compiler_params=pltpu.CompilerParams(vmem_limit_bytes=LIMIT),
        cost_estimate=pl.CostEstimate(
            flops=4 * tok * rows * blk, bytes_accessed=4 * (rows * blk + 2 * tok * blk), transcendentals=0
        ),
        name="input_term",
    )(jnp.reshape(which, (1,)), g_own, *g_other, *weights)


def project(a_all, weights, places, part, dtype, start=()):
    tok, depth = a_all.shape
    _, blk, cols = weights[places[0]].shape
    step = tok // 4
    n = len(places)

    def kernel(a_ref, *refs):
        out_ref, held, sem = refs[-3:]
        copies = [pltpu.make_async_copy(refs[k].at[part], held.at[k], sem.at[k]) for k in range(n)]

        @pl.when(pl.program_id(0) == 0)
        def _():
            for copy in copies:
                copy.start()
            for copy in copies:
                copy.wait()

        total = refs[n][...].astype(F32) if start else None
        for k, place in enumerate(places):
            term = dot(a_ref[:, place * blk:(place + 1) * blk], held[k], ((1,), (0,)))
            total = term if total is None else total + term
        out_ref[...] = total.astype(dtype)

    row_spec = pl.BlockSpec((step, cols), lambda i: (i, 0))
    return pl.pallas_call(
        kernel,
        grid=(4,),
        out_shape=jax.ShapeDtypeStruct((tok, cols), dtype),
        in_specs=[pl.BlockSpec((step, depth), lambda i: (i, 0))] + [HBM] * n + [row_spec] * len(start),
        out_specs=row_spec,
        scratch_shapes=[pltpu.VMEM((n, blk, cols), BF16), pltpu.SemaphoreType.DMA((n,))],
        compiler_params=pltpu.CompilerParams(vmem_limit_bytes=LIMIT),
        cost_estimate=pl.CostEstimate(
            flops=2 * tok * n * blk * cols, bytes_accessed=2 * n * blk * (tok + cols), transcendentals=0
        ),
        name="project",
    )(a_all, *(weights[place] for place in places), *start)


def per_device(activations, weight, cotangent):
    tok, blk = activations.shape
    part = weight.shape[0]
    c = lax.axis_index("depth")
    row, col = lax.axis_index("row"), lax.axis_index("col")
    z, xh, y, xl = row >> 1, row & 1, col >> 1, col & 1
    holder = (z & 1) == xl
    zero = jnp.int32(0)
    sign = 1 - 2 * c

    def first_of(core):
        return (jnp.where(holder, z, z + 2 * core - 1) & 3) >> 1

    def slot(block):
        block = block & 3
        core = block >> 1
        return jnp.where(core == c, 0, 2) + jnp.where((block & 1) == first_of(core), 0, 1)

    half = tok // 2
    from_opp = send(weight, to_x(2, True))
    from_lo = send(weight, to_x(1, False))
    from_hi = send(weight, to_x(-1, False))
    a_behind = send(activations, to_y(1))
    own_z = send(weight, to_z(1, None))
    own_first = jnp.where(holder, weight, after(own_z, from_opp))
    own_second = send(own_first, to_z(-1, 1))
    a_ahead = send(after(activations, from_opp, own_z), to_y(-1))
    g_upper, g_lower = cotangent[:half], cotangent[half:]
    from_opp, from_lo, from_hi, a_behind, own_first, own_second, g_upper = lax.optimization_barrier(
        (from_opp, from_lo, from_hi, a_behind, own_first, own_second, g_upper)
    )
    three = stack(xl, from_lo, from_hi, from_opp)
    three_z = send(three, to_z(1, None))
    a_opp = send(a_behind, to_y(1))
    g_upper = send(g_upper, to_xl)
    a_all = after(jnp.zeros((tok, 4 * blk), BF16), from_lo)
    for which, value in ((y, activations), (y - sign, a_behind), (y + sign, a_ahead), (y + 2, a_opp)):
        a_all = put(a_all, value, zero, slot(which) * blk)
    three_z, g_upper, g_lower, a_all = lax.optimization_barrier((three_z, g_upper, g_lower, a_all))

    def weight_term(first, g):
        return dot(a_all[:, first * blk:(first + 2) * blk], g, ((0,), (0,)))

    three_first = jnp.where(holder, three, three_z)
    three_second = send(three_first, to_z(-1, 1))
    g_lower = send(g_lower, to_xl)
    w_first = assemble(xh, own_first, three_first)
    w_first_x = send(w_first, to_core)
    wg_own_x = weight_term(2, after(cotangent, w_first)).astype(BF16)
    wg_own = weight_term(0, after(cotangent, wg_own_x))
    p_part = project(a_all, [w_first, None, w_first_x], (0, 2), 1, F32, ())
    three_second, g_lower, w_first_x, wg_own_x, wg_own, p_part = lax.optimization_barrier(
        (three_second, g_lower, w_first_x, wg_own_x, wg_own, p_part)
    )
    w_second = assemble(xh, own_second, three_second)
    w_second_x = send(w_second, to_core)
    weights = [w_first, w_second, w_first_x, w_second_x]

    wg_own_x = send(wg_own_x, to_core)
    g_other = jnp.concatenate([g_upper, g_lower])
    wg_other_x = weight_term(2, after(g_other, w_second)).astype(BF16)
    wg_own = (wg_own + after(wg_own_x, wg_other_x).astype(F32)).astype(BF16)
    wg_other_x = send(wg_other_x, to_core)
    wg_own_s = jnp.where(holder, wg_own[blk:], wg_own[:blk])
    wg_own_a = send(wg_own_s, to_z(1, -1))

    def d_block(which, *before):
        return input_term(slot(which), after(cotangent, *before), (g_upper, g_lower), weights)

    w_then = [None, after(w_second, wg_own_s), None, w_second_x]
    p_term = project(a_all, w_then, (1, 3), 1, BF16, (p_part,))
    p_other = send(p_term, to_xl)

    d_opp = d_block(y + 2, p_term)
    d_a = send(d_opp, to_y(1))
    wg_other = weight_term(0, after(g_other, d_opp))
    wg_other = (wg_other + wg_other_x.astype(F32)).astype(BF16)
    wg_other_s = jnp.where(holder, wg_other[blk:], wg_other[:blk])
    wg_other_a = send(wg_other_s, to_z(1, -1))
    wg_own_t = add(wg_own[blk:], after(wg_own_a, wg_other_s))
    wg_own_b = send(wg_own_t, to_z(None, 1))
    d_behind = d_block(y - sign, wg_own_t)
    d_ahead = d_block(y + sign, d_behind)
    d_behind = after(d_behind, d_a, d_ahead)
    d_b = send(d_behind, to_y(-1))
    wg_other_t = add(wg_other[blk:], after(wg_other_a, d_behind))
    wg_other_b = send(wg_other_t, to_z(None, 1))
    d_own = d_block(y, wg_other_t)
    d_c_term = add(d_ahead, after(d_a, d_b, p_other, d_own))
    d_c = send(d_c_term, to_y(1))

    kept_own = add(wg_own[:blk], wg_own_a, after(wg_own_b, d_c_term))
    opp_tile = cut(kept_own, (1 - xh) * part, zero, part, blk)
    own_tile = cut(kept_own, xh * part, zero, part, blk)
    got_opp = send(opp_tile, to_x(2, True))
    kept_other = add(wg_other[:blk], wg_other_a, after(wg_other_b, opp_tile))
    up = xh ^ xl
    got_lo = send(cut(kept_other, up * part, zero, part, blk), to_x(1, True))
    got_hi = send(cut(kept_other, (1 - up) * part, zero, part, blk), to_x(-1, True))
    w_then = [after(weights[0], d_own)] + weights[1:]
    projected = project(a_all, w_then, (0, 1, 2, 3), 0, BF16, (p_other,))
    grad_input = add(d_own, d_b, d_c)
    got_opp, got_lo, got_hi = (after(got, projected, grad_input) for got in (got_opp, got_lo, got_hi))
    scaling = 1.0 / math.sqrt(tok * lax.axis_size("depth") * lax.axis_size("row"))
    total = jnp.where(
        holder,
        own_tile.astype(F32) + got_opp.astype(F32),
        got_lo.astype(F32) + got_hi.astype(F32),
    )
    grad_weight = (total * scaling).astype(BF16)
    return (projected, grad_input, grad_weight)


def solution(mesh):
    spec = P(("depth", "row"), "col")
    return jax.shard_map(
        per_device, mesh=mesh, in_specs=(spec,) * 3, out_specs=(spec,) * 3, check_vma=False
    )
```

```python
import math

import jax
import jax.numpy as jnp
from jax import lax
from jax.experimental import pallas as pl
from jax.experimental.pallas import tpu as pltpu
from jax.sharding import PartitionSpec as P

AXES = ("depth", "row", "col")
F32, BF16 = jnp.float32, jnp.bfloat16


def send(value, target):
    pairs = []
    for c in range(2):
        for z in range(4):
            for xh in range(2):
                for y in range(4):
                    for xl in range(2):
                        to = target(c, z, xh, y, xl)
                        if to is not None:
                            tc, tz, txh, ty, txl = to
                            dst = tc * 64 + (tz % 4 * 2 + txh % 2) * 8 + ty % 4 * 2 + txl % 2
                            pairs.append((c * 64 + (z * 2 + xh) * 8 + y * 2 + xl, dst))
    return lax.ppermute(value, AXES, pairs)


def to_core(c, z, xh, y, xl):
    return (1 - c, z, xh, y, xl)


def to_y(step):
    return lambda c, z, xh, y, xl: (c, z, xh, y + step * (1 - 2 * c), xl)


def to_z(holders, others):
    def target(c, z, xh, y, xl):
        step = holders if z % 2 == xl else others
        return None if step is None else (c, z + step * (1 - 2 * c), xh, y, xl)

    return target


def to_x(step, holders):
    def target(c, z, xh, y, xl):
        if (z % 2 == xl) != holders:
            return None
        x = (2 * xh + xl + step) % 4
        return (c, z, x // 2, y, x % 2)

    return target


def to_xl(c, z, xh, y, xl):
    return (c, z, xh, y, 1 - xl)


def dot(a, b, dims):
    return lax.dot_general(a, b, (dims, ((), ())), preferred_element_type=F32)


def add(*terms):
    total = terms[0].astype(F32)
    for term in terms[1:]:
        total = total + term.astype(F32)
    return total.astype(BF16)


def after(value, *others):
    return lax.optimization_barrier((value,) + others)[0]


def put(buffer, value, row, col):
    return lax.dynamic_update_slice(buffer, value, (row, col))


def cut(value, row, col, rows, cols):
    return lax.dynamic_slice(value, (row, col), (rows, cols))


VMEM = pl.BlockSpec(memory_space=pltpu.VMEM)
SMEM = pl.BlockSpec(memory_space=pltpu.SMEM)
ANY = pl.BlockSpec(memory_space=pl.ANY)
HBM = pl.BlockSpec(memory_space=pltpu.HBM)
LIMIT = 13 * 2**20


def local(kernel, out_shape, in_specs, out_spec, moved, name, aliases=None, scratch=()):
    return pl.pallas_call(
        kernel,
        out_shape=jax.ShapeDtypeStruct(out_shape, BF16),
        in_specs=in_specs,
        out_specs=out_spec,
        scratch_shapes=scratch,
        input_output_aliases=aliases or {},
        compiler_params=pltpu.CompilerParams(vmem_limit_bytes=LIMIT),
        cost_estimate=pl.CostEstimate(flops=0, bytes_accessed=moved, transcendentals=0),
        name=name,
    )


def stack(xl, from_lo, from_hi, from_opp):
    rows, cols = from_lo.shape

    def kernel(xl_ref, lo_ref, hi_ref, opp_ref, out_ref):
        for value, (near, far) in enumerate(((hi_ref, lo_ref), (lo_ref, hi_ref))):

            @pl.when(xl_ref[0] == value)
            def _():
                out_ref[0] = near[...]
                out_ref[1] = far[...]

        out_ref[2] = opp_ref[...]

    call = local(kernel, (3, rows, cols), [SMEM] + [VMEM] * 3, VMEM, 12 * rows * cols, "stack")
    return call(jnp.reshape(xl, (1,)), from_lo, from_hi, from_opp)


def choose(first, one, two):
    def kernel(first_ref, one_ref, two_ref, out_ref, sem):
        @pl.when(first_ref[0] == 1)
        def _():
            copy = pltpu.make_async_copy(one_ref, out_ref, sem)
            copy.start()
            copy.wait()

    call = local(
        kernel, one.shape, [SMEM, HBM, HBM], HBM, 4 * one.size, "choose", {2: 0}, (pltpu.SemaphoreType.DMA,)
    )
    return call(jnp.reshape(first.astype(jnp.int32), (1,)), one, two)


def assemble(xh, own, three):
    rows, cols = own.shape

    def kernel(xh_ref, own_ref, three_ref, out_ref, sem):
        for value in range(2):
            upper = pl.ds(value * rows, rows)
            lower = pl.ds((1 - value) * rows, rows)

            @pl.when(xh_ref[0] == value)
            def _():
                pairs = (
                    (own_ref, out_ref.at[0, upper]),
                    (three_ref.at[2], out_ref.at[0, lower]),
                    (three_ref.at[0], out_ref.at[1, upper]),
                    (three_ref.at[1], out_ref.at[1, lower]),
                )
                copies = [pltpu.make_async_copy(*pair, sem.at[k]) for k, pair in enumerate(pairs)]
                for copy in copies:
                    copy.start()
                for copy in copies:
                    copy.wait()

    call = local(
        kernel, (2, 2 * rows, cols), [SMEM, ANY, ANY], HBM, 16 * rows * cols, "assemble", None,
        (pltpu.SemaphoreType.DMA((4,)),)
    )
    return call(jnp.reshape(xh, (1,)), own, three)


def input_term(which, g_own, g_other, weights):
    tok, blk = g_own.shape
    _, rows, _ = weights[0].shape
    step = tok // 4
    n = len(weights)

    def kernel(which_ref, g_own_ref, upper_ref, lower_ref, *refs):
        out_ref, held, sem = refs[n:]
        half = pl.program_id(0) // 2

        @pl.when(pl.program_id(0) == 0)
        def _():
            for place in range(n):

                @pl.when(which_ref[0] == place)
                def _():
                    copy = pltpu.make_async_copy(refs[place], held, sem)
                    copy.start()
                    copy.wait()

        g_other_block = jnp.where(half == 0, upper_ref[...], lower_ref[...])
        total = dot(g_own_ref[...], held[0], ((1,), (1,)))
        total += dot(g_other_block, held[1], ((1,), (1,)))
        out_ref[...] = total.astype(BF16)

    g_spec = pl.BlockSpec((step, blk), lambda i: (i, 0))
    upper_spec = pl.BlockSpec((step, blk), lambda i: (jnp.minimum(i, 1), 0))
    lower_spec = pl.BlockSpec((step, blk), lambda i: (jnp.maximum(i - 2, 0), 0))
    return pl.pallas_call(
        kernel,
        grid=(4,),
        out_shape=jax.ShapeDtypeStruct((tok, rows), BF16),
        in_specs=[SMEM, g_spec, upper_spec, lower_spec] + [HBM] * n,
        out_specs=g_spec,
        scratch_shapes=[pltpu.VMEM((2, rows, blk), BF16), pltpu.SemaphoreType.DMA],
        compiler_params=pltpu.CompilerParams(vmem_limit_bytes=LIMIT),
        cost_estimate=pl.CostEstimate(
            flops=4 * tok * rows * blk, bytes_accessed=4 * (rows * blk + 2 * tok * blk), transcendentals=0
        ),
        name="input_term",
    )(jnp.reshape(which, (1,)), g_own, *g_other, *weights)


def project(a_all, weights, places, part, dtype, start=()):
    tok, depth = a_all.shape
    _, blk, cols = weights[places[0]].shape
    step = tok // 4
    n = len(places)

    def kernel(a_ref, *refs):
        out_ref, held, sem = refs[-3:]
        copies = [pltpu.make_async_copy(refs[k].at[part], held.at[k], sem.at[k]) for k in range(n)]

        @pl.when(pl.program_id(0) == 0)
        def _():
            for copy in copies:
                copy.start()
            for copy in copies:
                copy.wait()

        total = refs[n][...].astype(F32) if start else None
        for k, place in enumerate(places):
            term = dot(a_ref[:, place * blk:(place + 1) * blk], held[k], ((1,), (0,)))
            total = term if total is None else total + term
        out_ref[...] = total.astype(dtype)

    row_spec = pl.BlockSpec((step, cols), lambda i: (i, 0))
    return pl.pallas_call(
        kernel,
        grid=(4,),
        out_shape=jax.ShapeDtypeStruct((tok, cols), dtype),
        in_specs=[pl.BlockSpec((step, depth), lambda i: (i, 0))] + [HBM] * n + [row_spec] * len(start),
        out_specs=row_spec,
        scratch_shapes=[pltpu.VMEM((n, blk, cols), BF16), pltpu.SemaphoreType.DMA((n,))],
        compiler_params=pltpu.CompilerParams(vmem_limit_bytes=LIMIT),
        cost_estimate=pl.CostEstimate(
            flops=2 * tok * n * blk * cols, bytes_accessed=2 * n * blk * (tok + cols), transcendentals=0
        ),
        name="project",
    )(a_all, *(weights[place] for place in places), *start)


def per_device(activations, weight, cotangent):
    tok, blk = activations.shape
    part = weight.shape[0]
    c = lax.axis_index("depth")
    row, col = lax.axis_index("row"), lax.axis_index("col")
    z, xh, y, xl = row >> 1, row & 1, col >> 1, col & 1
    holder = (z & 1) == xl
    zero = jnp.int32(0)
    sign = 1 - 2 * c

    def first_of(core):
        return (jnp.where(holder, z, z + 2 * core - 1) & 3) >> 1

    def slot(block):
        block = block & 3
        core = block >> 1
        return jnp.where(core == c, 0, 2) + jnp.where((block & 1) == first_of(core), 0, 1)

    half = tok // 2
    from_opp = send(weight, to_x(2, True))
    from_lo = send(weight, to_x(1, False))
    from_hi = send(weight, to_x(-1, False))
    a_behind = send(activations, to_y(1))
    own_z = send(weight, to_z(1, None))
    own_first = jnp.where(holder, weight, after(own_z, from_opp))
    own_second = send(own_first, to_z(-1, 1))
    a_ahead = send(after(activations, from_opp, own_z), to_y(-1))
    g_upper, g_lower = cotangent[:half], cotangent[half:]
    from_opp, from_lo, from_hi, a_behind, own_first, own_second, g_upper = lax.optimization_barrier(
        (from_opp, from_lo, from_hi, a_behind, own_first, own_second, g_upper)
    )
    three = stack(xl, from_lo, from_hi, from_opp)
    three_z = send(three, to_z(1, None))
    a_opp = send(a_behind, to_y(1))
    g_upper = send(g_upper, to_xl)
    a_all = after(jnp.zeros((tok, 4 * blk), BF16), from_lo)
    for which, value in ((y, activations), (y - sign, a_behind), (y + sign, a_ahead), (y + 2, a_opp)):
        a_all = put(a_all, value, zero, slot(which) * blk)
    three_z, g_upper, g_lower, a_all = lax.optimization_barrier((three_z, g_upper, g_lower, a_all))

    def weight_term(first, g):
        return dot(a_all[:, first * blk:(first + 2) * blk], g, ((0,), (0,)))

    three_first = jnp.where(holder, three, three_z)
    three_second = send(three_first, to_z(-1, 1))
    g_lower = send(g_lower, to_xl)
    w_first = assemble(xh, own_first, three_first)
    w_first_x = send(w_first, to_core)
    wg_own_x = weight_term(2, after(cotangent, w_first, w_first_x)).astype(BF16)
    wg_own = weight_term(0, after(cotangent, wg_own_x))
    p_part = project(a_all, [w_first, None, w_first_x], (0, 2), 1, F32, ())
    three_second, g_lower, w_first_x, wg_own_x, wg_own, p_part = lax.optimization_barrier(
        (three_second, g_lower, w_first_x, wg_own_x, wg_own, p_part)
    )
    w_second = assemble(xh, own_second, three_second)
    w_second_x = send(w_second, to_core)
    weights = [w_first, w_second, w_first_x, w_second_x]

    wg_own_x = send(wg_own_x, to_core)
    g_other = jnp.concatenate([g_upper, g_lower])
    wg_other_x = weight_term(2, after(g_other, w_second)).astype(BF16)
    wg_own = (wg_own + after(wg_own_x, wg_other_x).astype(F32)).astype(BF16)
    wg_other_x = send(wg_other_x, to_core)
    wg_own_s = jnp.where(holder, wg_own[blk:], wg_own[:blk])
    wg_own_a = send(wg_own_s, to_z(1, -1))

    def d_block(which, *before):
        return input_term(slot(which), after(cotangent, *before), (g_upper, g_lower), weights)

    d_opp = d_block(y + 2, wg_own_s)
    d_a = send(d_opp, to_y(1))

    w_then = [None, after(w_second, d_opp), None, w_second_x]
    p_term = project(a_all, w_then, (1, 3), 1, BF16, (p_part,))
    p_other = send(p_term, to_xl)

    wg_other = weight_term(0, after(g_other, p_term))
    wg_other = (wg_other + wg_other_x.astype(F32)).astype(BF16)
    wg_other_s = jnp.where(holder, wg_other[blk:], wg_other[:blk])
    wg_other_a = send(wg_other_s, to_z(1, -1))
    wg_own_t = add(wg_own[blk:], after(wg_own_a, wg_other_s))
    wg_own_b = send(wg_own_t, to_z(None, 1))
    d_behind = d_block(y - sign, wg_own_t)
    d_ahead = d_block(y + sign, d_behind)
    d_behind = after(d_behind, d_a, d_ahead)
    d_b = send(d_behind, to_y(-1))
    wg_other_t = add(wg_other[blk:], after(wg_other_a, d_behind))
    wg_other_b = send(wg_other_t, to_z(None, 1))
    d_own = d_block(y, wg_other_t)
    d_c_term = add(d_ahead, after(d_a, d_b, p_other, d_own))
    d_c = send(d_c_term, to_y(1))

    kept_own = add(wg_own[:blk], wg_own_a, after(wg_own_b, d_c_term))
    opp_tile = cut(kept_own, (1 - xh) * part, zero, part, blk)
    own_tile = cut(kept_own, xh * part, zero, part, blk)
    got_opp = send(opp_tile, to_x(2, True))
    kept_other = add(wg_other[:blk], wg_other_a, after(wg_other_b, opp_tile))
    up = xh ^ xl
    got_lo = send(cut(kept_other, up * part, zero, part, blk), to_x(1, True))
    got_hi = send(cut(kept_other, (1 - up) * part, zero, part, blk), to_x(-1, True))
    w_then = [after(weights[0], d_own)] + weights[1:]
    projected = project(a_all, w_then, (0, 1, 2, 3), 0, BF16, (p_other,))
    grad_input = add(d_own, d_b, d_c)
    got_opp, got_lo, got_hi = (after(got, projected, grad_input) for got in (got_opp, got_lo, got_hi))
    scaling = 1.0 / math.sqrt(tok * lax.axis_size("depth") * lax.axis_size("row"))
    total = jnp.where(
        holder,
        own_tile.astype(F32) + got_opp.astype(F32),
        got_lo.astype(F32) + got_hi.astype(F32),
    )
    grad_weight = (total * scaling).astype(BF16)
    return (projected, grad_input, grad_weight)


def solution(mesh):
    spec = P(("depth", "row"), "col")
    return jax.shard_map(
        per_device, mesh=mesh, in_specs=(spec,) * 3, out_specs=(spec,) * 3, check_vma=False
    )
```

```python
import math

import jax
import jax.numpy as jnp
from jax import lax
from jax.experimental import pallas as pl
from jax.experimental.pallas import tpu as pltpu
from jax.sharding import PartitionSpec as P

AXES = ("depth", "row", "col")
F32, BF16 = jnp.float32, jnp.bfloat16


def send(value, target):
    pairs = []
    for c in range(2):
        for z in range(4):
            for xh in range(2):
                for y in range(4):
                    for xl in range(2):
                        to = target(c, z, xh, y, xl)
                        if to is not None:
                            tc, tz, txh, ty, txl = to
                            dst = tc * 64 + (tz % 4 * 2 + txh % 2) * 8 + ty % 4 * 2 + txl % 2
                            pairs.append((c * 64 + (z * 2 + xh) * 8 + y * 2 + xl, dst))
    return lax.ppermute(value, AXES, pairs)


def to_core(c, z, xh, y, xl):
    return (1 - c, z, xh, y, xl)


def to_y(step):
    return lambda c, z, xh, y, xl: (c, z, xh, y + step * (1 - 2 * c), xl)


def to_z(holders, others):
    def target(c, z, xh, y, xl):
        step = holders if z % 2 == xl else others
        return None if step is None else (c, z + step * (1 - 2 * c), xh, y, xl)

    return target


def to_x(step, holders):
    def target(c, z, xh, y, xl):
        if (z % 2 == xl) != holders:
            return None
        x = (2 * xh + xl + step) % 4
        return (c, z, x // 2, y, x % 2)

    return target


def to_xl(c, z, xh, y, xl):
    return (c, z, xh, y, 1 - xl)


def dot(a, b, dims):
    return lax.dot_general(a, b, (dims, ((), ())), preferred_element_type=F32)


def add(*terms):
    total = terms[0].astype(F32)
    for term in terms[1:]:
        total = total + term.astype(F32)
    return total.astype(BF16)


def after(value, *others):
    return lax.optimization_barrier((value,) + others)[0]


def put(buffer, value, row, col):
    return lax.dynamic_update_slice(buffer, value, (row, col))


def cut(value, row, col, rows, cols):
    return lax.dynamic_slice(value, (row, col), (rows, cols))


VMEM = pl.BlockSpec(memory_space=pltpu.VMEM)
SMEM = pl.BlockSpec(memory_space=pltpu.SMEM)
ANY = pl.BlockSpec(memory_space=pl.ANY)
HBM = pl.BlockSpec(memory_space=pltpu.HBM)
LIMIT = 13 * 2**20


def local(kernel, out_shape, in_specs, out_spec, moved, name, aliases=None, scratch=()):
    return pl.pallas_call(
        kernel,
        out_shape=jax.ShapeDtypeStruct(out_shape, BF16),
        in_specs=in_specs,
        out_specs=out_spec,
        scratch_shapes=scratch,
        input_output_aliases=aliases or {},
        compiler_params=pltpu.CompilerParams(vmem_limit_bytes=LIMIT),
        cost_estimate=pl.CostEstimate(flops=0, bytes_accessed=moved, transcendentals=0),
        name=name,
    )


def stack(xl, from_lo, from_hi, from_opp):
    rows, cols = from_lo.shape

    def kernel(xl_ref, lo_ref, hi_ref, opp_ref, out_ref):
        for value, (near, far) in enumerate(((hi_ref, lo_ref), (lo_ref, hi_ref))):

            @pl.when(xl_ref[0] == value)
            def _():
                out_ref[0] = near[...]
                out_ref[1] = far[...]

        out_ref[2] = opp_ref[...]

    call = local(kernel, (3, rows, cols), [SMEM] + [VMEM] * 3, VMEM, 12 * rows * cols, "stack")
    return call(jnp.reshape(xl, (1,)), from_lo, from_hi, from_opp)


def choose(first, one, two):
    def kernel(first_ref, one_ref, two_ref, out_ref, sem):
        @pl.when(first_ref[0] == 1)
        def _():
            copy = pltpu.make_async_copy(one_ref, out_ref, sem)
            copy.start()
            copy.wait()

    call = local(
        kernel, one.shape, [SMEM, HBM, HBM], HBM, 4 * one.size, "choose", {2: 0}, (pltpu.SemaphoreType.DMA,)
    )
    return call(jnp.reshape(first.astype(jnp.int32), (1,)), one, two)


def assemble(xh, own, three):
    rows, cols = own.shape

    def kernel(xh_ref, own_ref, three_ref, out_ref, sem):
        for value in range(2):
            upper = pl.ds(value * rows, rows)
            lower = pl.ds((1 - value) * rows, rows)

            @pl.when(xh_ref[0] == value)
            def _():
                pairs = (
                    (own_ref, out_ref.at[0, upper]),
                    (three_ref.at[2], out_ref.at[0, lower]),
                    (three_ref.at[0], out_ref.at[1, upper]),
                    (three_ref.at[1], out_ref.at[1, lower]),
                )
                copies = [pltpu.make_async_copy(*pair, sem.at[k]) for k, pair in enumerate(pairs)]
                for copy in copies:
                    copy.start()
                for copy in copies:
                    copy.wait()

    call = local(
        kernel, (2, 2 * rows, cols), [SMEM, ANY, ANY], HBM, 16 * rows * cols, "assemble", None,
        (pltpu.SemaphoreType.DMA((4,)),)
    )
    return call(jnp.reshape(xh, (1,)), own, three)


def input_term(which, g_own, g_other, weights):
    tok, blk = g_own.shape
    _, rows, _ = weights[0].shape
    step = tok // 4
    n = len(weights)

    def kernel(which_ref, g_own_ref, upper_ref, lower_ref, *refs):
        out_ref, held, sem = refs[n:]
        half = pl.program_id(0) // 2

        @pl.when(pl.program_id(0) == 0)
        def _():
            for place in range(n):

                @pl.when(which_ref[0] == place)
                def _():
                    for k in range(2):
                        pltpu.make_async_copy(refs[place].at[k], held.at[k], sem.at[k]).start()

        def arrived(k):
            @pl.when(pl.program_id(0) == 0)
            def _():
                pltpu.make_async_copy(refs[0].at[k], held.at[k], sem.at[k]).wait()

        g_other_block = jnp.where(half == 0, upper_ref[...], lower_ref[...])
        arrived(0)
        total = dot(g_own_ref[...], held[0], ((1,), (1,)))
        arrived(1)
        total += dot(g_other_block, held[1], ((1,), (1,)))
        out_ref[...] = total.astype(BF16)

    g_spec = pl.BlockSpec((step, blk), lambda i: (i, 0))
    upper_spec = pl.BlockSpec((step, blk), lambda i: (jnp.minimum(i, 1), 0))
    lower_spec = pl.BlockSpec((step, blk), lambda i: (jnp.maximum(i - 2, 0), 0))
    return pl.pallas_call(
        kernel,
        grid=(4,),
        out_shape=jax.ShapeDtypeStruct((tok, rows), BF16),
        in_specs=[SMEM, g_spec, upper_spec, lower_spec] + [HBM] * n,
        out_specs=g_spec,
        scratch_shapes=[pltpu.VMEM((2, rows, blk), BF16), pltpu.SemaphoreType.DMA((2,))],
        compiler_params=pltpu.CompilerParams(vmem_limit_bytes=LIMIT),
        cost_estimate=pl.CostEstimate(
            flops=4 * tok * rows * blk, bytes_accessed=4 * (rows * blk + 2 * tok * blk), transcendentals=0
        ),
        name="input_term",
    )(jnp.reshape(which, (1,)), g_own, *g_other, *weights)


def project(a_all, weights, places, part, dtype, start=()):
    tok, depth = a_all.shape
    _, blk, cols = weights[places[0]].shape
    step = tok // 4
    n = len(places)

    def kernel(a_ref, *refs):
        out_ref, held, sem = refs[-3:]
        copies = [pltpu.make_async_copy(refs[k].at[part], held.at[k], sem.at[k]) for k in range(n)]

        @pl.when(pl.program_id(0) == 0)
        def _():
            for copy in copies:
                copy.start()

        def arrived(k):
            @pl.when(pl.program_id(0) == 0)
            def _():
                copies[k].wait()

        total = refs[n][...].astype(F32) if start else None
        for k, place in enumerate(places):
            arrived(k)
            term = dot(a_ref[:, place * blk:(place + 1) * blk], held[k], ((1,), (0,)))
            total = term if total is None else total + term
        out_ref[...] = total.astype(dtype)

    row_spec = pl.BlockSpec((step, cols), lambda i: (i, 0))
    return pl.pallas_call(
        kernel,
        grid=(4,),
        out_shape=jax.ShapeDtypeStruct((tok, cols), dtype),
        in_specs=[pl.BlockSpec((step, depth), lambda i: (i, 0))] + [HBM] * n + [row_spec] * len(start),
        out_specs=row_spec,
        scratch_shapes=[pltpu.VMEM((n, blk, cols), BF16), pltpu.SemaphoreType.DMA((n,))],
        compiler_params=pltpu.CompilerParams(vmem_limit_bytes=LIMIT),
        cost_estimate=pl.CostEstimate(
            flops=2 * tok * n * blk * cols, bytes_accessed=2 * n * blk * (tok + cols), transcendentals=0
        ),
        name="project",
    )(a_all, *(weights[place] for place in places), *start)


def per_device(activations, weight, cotangent):
    tok, blk = activations.shape
    part = weight.shape[0]
    c = lax.axis_index("depth")
    row, col = lax.axis_index("row"), lax.axis_index("col")
    z, xh, y, xl = row >> 1, row & 1, col >> 1, col & 1
    holder = (z & 1) == xl
    zero = jnp.int32(0)
    sign = 1 - 2 * c

    def first_of(core):
        return (jnp.where(holder, z, z + 2 * core - 1) & 3) >> 1

    def slot(block):
        block = block & 3
        core = block >> 1
        return jnp.where(core == c, 0, 2) + jnp.where((block & 1) == first_of(core), 0, 1)

    half = tok // 2
    from_opp = send(weight, to_x(2, True))
    from_lo = send(weight, to_x(1, False))
    from_hi = send(weight, to_x(-1, False))
    a_behind = send(activations, to_y(1))
    own_z = send(weight, to_z(1, None))
    own_first = jnp.where(holder, weight, after(own_z, from_opp))
    own_second = send(own_first, to_z(-1, 1))
    a_ahead = send(after(activations, from_opp, own_z), to_y(-1))
    g_upper, g_lower = cotangent[:half], cotangent[half:]
    from_opp, from_lo, from_hi, a_behind, own_first, own_second, g_upper = lax.optimization_barrier(
        (from_opp, from_lo, from_hi, a_behind, own_first, own_second, g_upper)
    )
    three = stack(xl, from_lo, from_hi, from_opp)
    three_z = send(three, to_z(1, None))
    a_opp = send(a_behind, to_y(1))
    g_upper = send(g_upper, to_xl)
    a_all = after(jnp.zeros((tok, 4 * blk), BF16), from_lo)
    for which, value in ((y, activations), (y - sign, a_behind), (y + sign, a_ahead), (y + 2, a_opp)):
        a_all = put(a_all, value, zero, slot(which) * blk)
    three_z, g_upper, g_lower, a_all = lax.optimization_barrier((three_z, g_upper, g_lower, a_all))

    def weight_term(first, g):
        return dot(a_all[:, first * blk:(first + 2) * blk], g, ((0,), (0,)))

    three_first = jnp.where(holder, three, three_z)
    three_second = send(three_first, to_z(-1, 1))
    g_lower = send(g_lower, to_xl)
    w_first = assemble(xh, own_first, three_first)
    w_first_x = send(w_first, to_core)
    wg_own_x = weight_term(2, after(cotangent, w_first, w_first_x)).astype(BF16)
    wg_own = weight_term(0, after(cotangent, wg_own_x))
    p_part = project(a_all, [w_first, None, w_first_x], (0, 2), 1, F32, ())
    three_second, g_lower, w_first_x, wg_own_x, wg_own, p_part = lax.optimization_barrier(
        (three_second, g_lower, w_first_x, wg_own_x, wg_own, p_part)
    )
    w_second = assemble(xh, own_second, three_second)
    w_second_x = send(w_second, to_core)
    weights = [w_first, w_second, w_first_x, w_second_x]

    wg_own_x = send(wg_own_x, to_core)
    g_other = jnp.concatenate([g_upper, g_lower])
    wg_other_x = weight_term(2, after(g_other, w_second)).astype(BF16)
    wg_own = (wg_own + after(wg_own_x, wg_other_x).astype(F32)).astype(BF16)
    wg_other_x = send(wg_other_x, to_core)
    wg_own_s = jnp.where(holder, wg_own[blk:], wg_own[:blk])
    wg_own_a = send(wg_own_s, to_z(1, -1))

    def d_block(which, *before):
        return input_term(slot(which), after(cotangent, *before), (g_upper, g_lower), weights)

    d_opp = d_block(y + 2, wg_own_s)
    d_a = send(d_opp, to_y(1))

    w_then = [None, after(w_second, d_opp), None, w_second_x]
    p_term = project(a_all, w_then, (1, 3), 1, BF16, (p_part,))
    p_other = send(p_term, to_xl)

    wg_other = weight_term(0, after(g_other, p_term))
    wg_other = (wg_other + wg_other_x.astype(F32)).astype(BF16)
    wg_other_s = jnp.where(holder, wg_other[blk:], wg_other[:blk])
    wg_other_a = send(wg_other_s, to_z(1, -1))
    wg_own_t = add(wg_own[blk:], after(wg_own_a, wg_other_s))
    wg_own_b = send(wg_own_t, to_z(None, 1))
    d_behind = d_block(y - sign, wg_own_t)
    d_ahead = d_block(y + sign, d_behind)
    d_behind = after(d_behind, d_a, d_ahead)
    d_b = send(d_behind, to_y(-1))
    wg_other_t = add(wg_other[blk:], after(wg_other_a, d_behind))
    wg_other_b = send(wg_other_t, to_z(None, 1))
    d_own = d_block(y, wg_other_t)
    d_c_term = add(d_ahead, after(d_a, d_b, p_other, d_own))
    d_c = send(d_c_term, to_y(1))

    kept_own = add(wg_own[:blk], wg_own_a, after(wg_own_b, d_c_term))
    opp_tile = cut(kept_own, (1 - xh) * part, zero, part, blk)
    own_tile = cut(kept_own, xh * part, zero, part, blk)
    got_opp = send(opp_tile, to_x(2, True))
    kept_other = add(wg_other[:blk], wg_other_a, after(wg_other_b, opp_tile))
    up = xh ^ xl
    got_lo = send(cut(kept_other, up * part, zero, part, blk), to_x(1, True))
    got_hi = send(cut(kept_other, (1 - up) * part, zero, part, blk), to_x(-1, True))
    w_then = [after(weights[0], d_own)] + weights[1:]
    projected = project(a_all, w_then, (0, 1, 2, 3), 0, BF16, (p_other,))
    grad_input = add(d_own, d_b, d_c)
    got_opp, got_lo, got_hi = (after(got, projected, grad_input) for got in (got_opp, got_lo, got_hi))
    scaling = 1.0 / math.sqrt(tok * lax.axis_size("depth") * lax.axis_size("row"))
    total = jnp.where(
        holder,
        own_tile.astype(F32) + got_opp.astype(F32),
        got_lo.astype(F32) + got_hi.astype(F32),
    )
    grad_weight = (total * scaling).astype(BF16)
    return (projected, grad_input, grad_weight)


def solution(mesh):
    spec = P(("depth", "row"), "col")
    return jax.shard_map(
        per_device, mesh=mesh, in_specs=(spec,) * 3, out_specs=(spec,) * 3, check_vma=False
    )
```
